256 devices in a mesh: mem: 32 (over z, x), head: 8 (over y, core).
Axes of the slice: x: 4, y: 4, z: 8, core: 2. Of those that a mesh axis runs over, the one named last changes fastest.
Arguments:
- query_rows: bfloat16 [32, 1024, 4096], P('mem', 'head'), may hold values from -6 to 6
- key_rows: bfloat16 [32, 1024, 4096], P('mem', 'head'), may hold values from -6 to 6
- value_rows: bfloat16 [32, 1024, 4096], P('mem', 'head'), may hold values from -6 to 6
- memory_keys: bfloat16 [256, 128, 4096], P('mem', None, 'head'), may hold values from -6 to 6
- memory_values: bfloat16 [256, 128, 4096], P('mem', None, 'head'), may hold values from -6 to 6
- owner_list: int32 [32, 8, 2], P('mem'), may hold values from 0 to 31, all different within a row; in each aligned block of 8 rows (0 to 7, 8 to 15, ..., all dimensions but the last counted through in order) at most 2 rows name the same one
- slot_list: int32 [32, 8, 2], P('mem'), may hold values from 0 to 7
- gate_logit: float32 [32], P('head'), may hold values from -2 to 2
Outputs:
- mixed_out: bfloat16 [32, 1024, 4096], P('mem', 'head')
The draws below stay inside these ranges and needn't reach their ends.
Inputs may be any that keep to these rules, and one draw needn't show every extreme that they name: `owner_list`: the 2 entries of one query block name different indices; among the 8 query blocks of one segment, no index is named more than 2 times.
All inputs are finite; a program needn't handle non-finite values.
Results may differ from the reference program's by a relative error of at most 0.012.
Values may be sent and summed in bfloat16 or wider, within the bound.
No kernel may reach another device: no remote copies, remote signals or barrier semaphores. Data moves between devices by JAX's collectives and lax.ppermute only.
A program may use at most 128 MiB of HBM per device.

```python
import math
import jax
import jax.numpy as jnp
import numpy as np
from jax import lax

H = 32
DH = 128
D = 4096
BLK = 128
TOPK = 2
CAP = 2
MB_DEV = 8
LEN = 1024
QBLOCKS = 8
SEQS = 32
NB = 256
N_MEM = 32


def drawn_field(key, array_shape):
    return jax.random.truncated_normal(key, -6.0, 6.0, array_shape, jnp.float32)


def draw_query_rows(key, part):
    key = jax.random.fold_in(key, 11)
    samples = drawn_field(key, (SEQS, LEN, D))
    return samples.astype(jnp.bfloat16)


def draw_key_rows(key, part):
    key = jax.random.fold_in(key, 23)
    samples = drawn_field(key, (SEQS, LEN, D))
    return samples.astype(jnp.bfloat16)


def draw_memory_keys(key, part):
    key = jax.random.fold_in(key, 37)
    samples = drawn_field(key, (NB, BLK, D))
    return samples.astype(jnp.bfloat16)


def plant(result, own_key, smallest, top_value):
    longest = result.shape.index(max(result.shape))
    spots = []
    for shift in (0, 1):
        where = [jax.random.randint(jax.random.fold_in(own_key, axis), (), 0, length) for axis, length in enumerate(result.shape)]
        where[longest] = (where[longest] + shift) % result.shape[longest]
        spots.append(tuple(where))
    return result.at[spots[0]].set(smallest).at[spots[1]].set(top_value)


def block_scale(key, dims, cuts, least, top_value):
    def one(position, blocks):
        draws = jax.random.uniform(jax.random.fold_in(jax.random.fold_in(key, 6), position), (blocks,), jnp.float32, least / len(cuts), top_value / len(cuts))
        return jnp.repeat(jnp.exp(draws), dims[position] // blocks).reshape((-1,) + (1,) * (len(dims) - position - 1))

    loudness = one(*cuts[0])
    for cut in cuts[1:]:
        loudness = loudness * one(*cut)
    return loudness


def shared_out(rng, own, number, rows, amount, top, limit, lean):
    ranking = jax.random.permutation(rng, amount)
    packed, ordinary = load_shares(amount, rows * top, limit, lean, True), load_shares(amount, rows * top, limit, lean, False)
    places = jnp.arange(amount)

    def named(sizes, offset_by):
        used = int((sizes > 0).sum())
        fixed = max(1, used // 4)
        passed = fixed + (places - fixed + offset_by * (used - fixed)) % max(1, amount - fixed)
        return jnp.zeros((amount,), jnp.int32).at[ranking[jnp.where(places < fixed, places, passed)]].set(jnp.asarray(sizes, jnp.int32))

    sizes = jnp.where(number % 4 == 0, named(packed, number // 4), named(ordinary, number - number // 4 - 1))
    mixed = jax.random.permutation(jax.random.fold_in(own, 3), amount)
    donor, sink = mixed[0:amount // 2 * 2:2], mixed[1:amount // 2 * 2:2]
    room = jnp.minimum(sizes[donor] - 1, limit - sizes[sink]) // 2
    room = jnp.where((donor == ranking[0]) | (sink == ranking[0]) | (sizes[sink] == 0), 0, jnp.maximum(room, 0))
    passed = jax.random.randint(jax.random.fold_in(own, 4), (amount // 2,), 0, 1 << 20) % (room + 1)
    sizes = sizes.at[donor].add(-passed).at[sink].add(passed)
    members = jnp.searchsorted(jnp.cumsum(sizes), jnp.arange(rows * top), side="right").astype(jnp.int32)
    grid = members.reshape(top, rows).T
    grid = grid[jax.random.permutation(jax.random.fold_in(own, 1), rows)]
    offset_by = jax.random.randint(jax.random.fold_in(own, 2), (rows, 1), 0, top)
    return jnp.take_along_axis(grid, (jnp.arange(top)[None, :] + offset_by) % top, axis=1)


def load_shares(number_of, total, limit, slope, full):
    portions = [(1 << 20) // math.isqrt(rank ** slope) + 1 for rank in range(1, number_of + 1)]
    largest = limit if full else min(limit, max(-(-total // number_of), total * portions[0] // sum(portions)))
    least = 1 if total - largest >= number_of - 1 else 0
    holding, spare = [largest] + [least] * (number_of - 1), total - largest - least * (number_of - 1)
    while spare > 0:
        candidates = [i for i in range(1, number_of) if holding[i] < largest] or [i for i in range(1, number_of) if holding[i] < limit]
        whole, budget = sum([portions[i] for i in candidates]), spare
        for i in candidates:
            more = min(limit - holding[i], max(1, budget * portions[i] // whole), spare)
            holding[i] = holding[i] + more
            spare = spare - more
    return np.array(holding)


def centred(own_key, shape, deviation, bound, cuts=(), held_as=jnp.bfloat16):
    drawn = jax.random.normal(own_key, shape, jnp.float32) * deviation
    if len(cuts) > 0:
        drawn = block_scale(own_key, shape, cuts, -0.22, 0.18) * drawn
    return jnp.clip(drawn, min=-bound, max=bound).astype(held_as)


def setup_inputs(seed: int = 0) -> dict:
    key_list = jax.random.split(jax.random.key(seed), 9)
    query_rows = draw_query_rows(jax.random.fold_in(key_list[8], 71), 0)
    key_rows = draw_key_rows(jax.random.fold_in(key_list[8], 71), 0)
    value_rows = centred(key_list[2], (SEQS, LEN, D), 1.0, 6.0, ((0, 32), (1, 8)))
    memory_keys = draw_memory_keys(jax.random.fold_in(key_list[8], 71), 0)
    memory_values = centred(key_list[4], (NB, BLK, D), 1.0, 6.0, ((0, 32), (2, 8)))
    owner_list_keys = jax.random.split(jax.random.fold_in(key_list[5], 1), SEQS * QBLOCKS // QBLOCKS)
    owner_list_turns = jax.random.permutation(jax.random.fold_in(key_list[5], 3), SEQS * QBLOCKS // QBLOCKS)
    owner_list = jax.vmap(lambda own, number: shared_out(jax.random.fold_in(key_list[5], 2), own, number, QBLOCKS, N_MEM, TOPK, CAP, 2))(owner_list_keys, owner_list_turns).reshape((SEQS, QBLOCKS, TOPK))
    slot_list = plant(jax.random.randint(key_list[6], (SEQS, QBLOCKS, TOPK), 0, MB_DEV), jax.random.fold_in(key_list[6], 1), 0, MB_DEV - 1).astype(jnp.int32)
    gate_logit = jnp.clip(jax.random.uniform(key_list[7], (H,), jnp.float32, -2.0, 2.0) * block_scale(key_list[7], (H,), ((0, 8),), -0.4, 0.0), -2.0, 2.0)
    return dict(query_rows=query_rows, key_rows=key_rows, value_rows=value_rows, memory_keys=memory_keys, memory_values=memory_values, owner_list=owner_list, slot_list=slot_list, gate_logit=gate_logit)


negative_fill = -1e30


def local_attend(query_heads, key_heads, value_heads):
    block_rows = min(512, LEN)
    scaling = DH ** -0.5
    key_float = key_heads.astype(jnp.float32)
    value_float = value_heads.astype(jnp.float32)

    def one_block(number):
        offset = (number * block_rows).astype(jnp.int32)
        query_block = lax.dynamic_slice_in_dim(query_heads, offset, block_rows, 0).astype(jnp.float32)
        scores = jnp.einsum("qhd,khd->hqk", query_block, key_float) * scaling
        positions = offset + jnp.arange(block_rows, dtype=jnp.int32)
        allowed = jnp.arange(LEN, dtype=jnp.int32)[None, :] <= positions[:, None]
        scores = jnp.where(allowed[None], scores, negative_fill)
        weights = jax.nn.softmax(scores, axis=-1).astype(jnp.bfloat16)
        return jnp.einsum("hqk,khd->qhd", weights.astype(jnp.float32), value_float)

    pieces = lax.map(one_block, jnp.arange(LEN // block_rows, dtype=jnp.int32))
    return pieces.reshape(LEN, H, DH)


def memory_attend(query_blocks, fetched_keys, fetched_values):
    scaling = DH ** -0.5
    scores = jnp.einsum("bqhd,bkhd->bhqk", query_blocks.astype(jnp.float32), fetched_keys.astype(jnp.float32)) * scaling
    weights = jax.nn.softmax(scores, axis=-1).astype(jnp.bfloat16)
    return jnp.einsum("bhqk,bkhd->bqhd", weights.astype(jnp.float32), fetched_values.astype(jnp.float32))


def reference(query_rows, key_rows, value_rows, memory_keys, memory_values, owner_list, slot_list, gate_logit):
    gating = jax.nn.sigmoid(gate_logit.astype(jnp.float32))[None, :, None]

    def one_segment(inputs):
        query_seg, key_seg, value_seg, owner_ids, slot_ids = inputs
        query_heads = query_seg.reshape(LEN, H, DH)
        local_part = local_attend(query_heads, key_seg.reshape(LEN, H, DH), value_seg.reshape(LEN, H, DH))
        block_ids = (owner_ids * MB_DEV + slot_ids).reshape(-1).astype(jnp.int32)
        fetched_keys = memory_keys[block_ids].reshape(QBLOCKS, TOPK * BLK, H, DH)
        fetched_values = memory_values[block_ids].reshape(QBLOCKS, TOPK * BLK, H, DH)
        memory_part = memory_attend(query_heads.reshape(QBLOCKS, BLK, H, DH), fetched_keys, fetched_values)
        memory_part = memory_part.reshape(LEN, H, DH)
        combined = gating * memory_part + (1.0 - gating) * local_part
        return combined.reshape(LEN, D).astype(jnp.bfloat16)

    return lax.map(one_segment, (query_rows, key_rows, value_rows, owner_list, slot_list))
```

```python
import functools
import math

import jax
import jax.numpy as jnp
from jax import lax
from jax.experimental import pallas as pl
from jax.experimental.pallas import tpu as pltpu
from jax.sharding import PartitionSpec as P

DH = 128
BLK = 128
HEADS_DEV = 4
HEAD_DEVS = 8
MEM_DEVS = 32
SLOTS = 8
ROWS = 16
WIDTH = HEADS_DEV * DH
Q_TILE = 256
EXP_SCALE = math.log2(math.e) / math.sqrt(DH)
MASKED = -1e30

VMEM = pl.BlockSpec(memory_space=pltpu.VMEM)
SMEM = pl.BlockSpec(memory_space=pltpu.SMEM)


def params(mib):
    return pltpu.CompilerParams(vmem_limit_bytes=mib * 1024 * 1024)


def dot_nt(a, b):
    return lax.dot_general(a, b, (((1,), (1,)), ((), ())), preferred_element_type=jnp.float32)


def spread_kernel(keys_ref, values_ref, ids_ref, out_ref):
    for dest in range(MEM_DEVS):
        z, x = dest // HEADS_DEV, dest % HEADS_DEV
        rows, cols = pl.ds(z * ROWS, ROWS), pl.ds(x * DH, DH)
        out_ref[dest, 0:SLOTS] = keys_ref[:, rows, cols]
        out_ref[dest, SLOTS : 2 * SLOTS] = values_ref[:, rows, cols]
        out_ref[dest, 2 * SLOTS] = ids_ref[...]


def gather_kernel(ids_ref, table_ref, out_ref):
    def one(dest, carry):
        for k in range(2):
            block = ids_ref[2 * dest + k]
            owner, slot = block // SLOTS, block % SLOTS
            out_ref[dest, k, 0] = table_ref[owner, slot]
            out_ref[dest, k, 1] = table_ref[owner, SLOTS + slot]
        return carry

    lax.fori_loop(0, MEM_DEVS * HEAD_DEVS, one, 0, unroll=8)


def pack_kernel(me_ref, q_ref, k_ref, v_ref, *out_refs):
    for shift in range(HEAD_DEVS):
        dest = (me_ref[0] + shift) % HEAD_DEVS
        cols = pl.ds(pl.multiple_of(dest * WIDTH, WIDTH), WIDTH)
        for i, ref in enumerate((q_ref, k_ref, v_ref)):
            out_refs[shift][i] = ref[:, cols]


def local_kernel(me_ref, gate_ref, *refs):
    ins, outs = refs[:HEAD_DEVS], refs[HEAD_DEVS : 2 * HEAD_DEVS]
    held, result = refs[2 * HEAD_DEVS :]
    me = me_ref[0]
    for shift in range(HEAD_DEVS):
        held[:, (me + HEAD_DEVS - shift) % HEAD_DEVS] = ins[shift][...]
    length = HEAD_DEVS * BLK
    blocks = Q_TILE // BLK
    parts = []
    for j in range(HEADS_DEV):
        cols = pl.ds(j * DH, DH)
        gate = jax.nn.sigmoid(jnp.full((1, DH), gate_ref[j], jnp.float32))
        high = gate.astype(jnp.bfloat16)
        rest = gate - high.astype(jnp.float32)
        mid = rest.astype(jnp.bfloat16)
        low = (rest - mid.astype(jnp.float32)).astype(jnp.bfloat16)
        parts.append((high, mid, low))
        for tile in range(length // Q_TILE):
            rows = pl.ds(tile * blocks, blocks)
            query = held[0, rows, :, cols].reshape(Q_TILE, DH)
            diag = dot_nt(query, held[1, rows, :, cols].reshape(Q_TILE, DH))
            row_ids = lax.broadcasted_iota(jnp.int32, (Q_TILE, Q_TILE), 0)
            col_ids = lax.broadcasted_iota(jnp.int32, (Q_TILE, Q_TILE), 1)
            diag = jnp.where(col_ids <= row_ids, diag, MASKED)
            top = jnp.max(diag, axis=1, keepdims=True)
            if tile:
                before = pl.ds(0, tile * blocks)
                off = dot_nt(query, held[1, before, :, cols].reshape(tile * Q_TILE, DH))
                top = jnp.maximum(top, jnp.max(off, axis=1, keepdims=True))
            weights = jnp.exp2((diag - top) * EXP_SCALE)
            total = jnp.sum(weights, axis=1, keepdims=True)
            part = jnp.dot(
                weights.astype(jnp.bfloat16),
                held[2, rows, :, cols].reshape(Q_TILE, DH),
                preferred_element_type=jnp.float32,
            )
            if tile:
                weights = jnp.exp2((off - top) * EXP_SCALE)
                total = total + jnp.sum(weights, axis=1, keepdims=True)
                part = part + jnp.dot(
                    weights.astype(jnp.bfloat16),
                    held[2, before, :, cols].reshape(tile * Q_TILE, DH),
                    preferred_element_type=jnp.float32,
                )
            part = part * ((1.0 - gate) / total)
            result[rows, pl.ds(j * BLK, BLK), :] = part.astype(jnp.bfloat16).reshape(
                blocks, BLK, DH
            )
    tail = jnp.concatenate(
        [parts[j][i] for i in range(3) for j in range(HEADS_DEV)]
        + [jnp.zeros((ROWS - 3 * HEADS_DEV, DH), jnp.bfloat16)],
        axis=0,
    )
    for shift in range(HEAD_DEVS):
        outs[shift][pl.ds(0, WIDTH), :] = result[(me + shift) % HEAD_DEVS]
        outs[shift][pl.ds(WIDTH, ROWS), :] = tail


def mix_kernel(me_ref, q_ref, fetched_ref, *refs):
    ins, out_ref = refs[:HEAD_DEVS], refs[HEAD_DEVS]
    for shift in range(HEAD_DEVS):
        owner = (me_ref[0] + HEAD_DEVS - shift) % HEAD_DEVS
        tail = ins[shift][pl.ds(WIDTH, ROWS), :].astype(jnp.float32)
        for j in range(HEADS_DEV):
            cols = pl.ds(pl.multiple_of(owner * WIDTH + j * DH, DH), DH)
            keys = fetched_ref[:, j, owner, :, 0].reshape(2 * BLK, DH)
            values = fetched_ref[:, j, owner, :, 1].reshape(2 * BLK, DH)
            scores = dot_nt(q_ref[:, cols], keys)
            top = jnp.max(scores, axis=1, keepdims=True)
            weights = jnp.exp2((scores - top) * EXP_SCALE)
            total = jnp.sum(weights, axis=1, keepdims=True)
            part = jnp.dot(weights.astype(jnp.bfloat16), values, preferred_element_type=jnp.float32)
            gate = tail[j : j + 1] + tail[4 + j : 5 + j] + tail[8 + j : 9 + j]
            local = ins[shift][pl.ds(j * BLK, BLK), :].astype(jnp.float32)
            out_ref[:, cols] = (part * (gate / total) + local).astype(jnp.bfloat16)


def on_device(
    query_rows, key_rows, value_rows, memory_keys, memory_values, owner_list, slot_list, gate_logit
):
    me = lax.axis_index("head").astype(jnp.int32).reshape(1)

    def rotated(arrays):
        return [arrays[0]] + [
            lax.ppermute(
                arrays[s], "head", [(i, (i + s) % HEAD_DEVS) for i in range(HEAD_DEVS)]
            )
            for s in range(1, HEAD_DEVS)
        ]

    ids = (owner_list * SLOTS + slot_list).reshape(ROWS, 1)
    ids = jnp.broadcast_to(ids.astype(jnp.bfloat16), (ROWS, DH))
    spread = pl.pallas_call(
        spread_kernel,
        out_shape=jax.ShapeDtypeStruct((MEM_DEVS, 2 * SLOTS + 1, ROWS, DH), jnp.bfloat16),
        in_specs=[VMEM] * 3,
        out_specs=VMEM,
        compiler_params=params(24),
    )(memory_keys, memory_values, ids)
    table = lax.all_to_all(spread, "mem", split_axis=0, concat_axis=0, tiled=True)

    packed = pl.pallas_call(
        pack_kernel,
        out_shape=[jax.ShapeDtypeStruct((3, BLK, WIDTH), jnp.bfloat16)] * HEAD_DEVS,
        in_specs=[SMEM] + [VMEM] * 3,
        out_specs=[VMEM] * HEAD_DEVS,
        compiler_params=params(24),
    )(me, query_rows[0], key_rows[0], value_rows[0])
    packed = rotated(packed)
    local = pl.pallas_call(
        local_kernel,
        out_shape=[jax.ShapeDtypeStruct((WIDTH + ROWS, DH), jnp.bfloat16)] * HEAD_DEVS,
        in_specs=[SMEM, SMEM] + [VMEM] * HEAD_DEVS,
        out_specs=[VMEM] * HEAD_DEVS,
        scratch_shapes=[
            pltpu.VMEM((3, HEAD_DEVS, BLK, WIDTH), jnp.bfloat16),
            pltpu.VMEM((HEAD_DEVS, WIDTH, DH), jnp.bfloat16),
        ],
        compiler_params=params(32),
    )(me, gate_logit, *packed)
    local = rotated(local)

    all_ids = table[:, 2 * SLOTS, :, 0].astype(jnp.int32).reshape(MEM_DEVS * ROWS)
    requested = pl.pallas_call(
        gather_kernel,
        out_shape=jax.ShapeDtypeStruct((MEM_DEVS * HEAD_DEVS, 2, 2, ROWS, DH), jnp.bfloat16),
        in_specs=[SMEM, VMEM],
        out_specs=VMEM,
        compiler_params=params(24),
    )(all_ids, table)
    fetched = lax.all_to_all(requested, ("mem", "head"), split_axis=0, concat_axis=0, tiled=True)
    fetched = fetched.reshape(BLK // ROWS, HEADS_DEV, HEAD_DEVS, 2, 2, ROWS, DH)
    mixed = pl.pallas_call(
        mix_kernel,
        out_shape=jax.ShapeDtypeStruct((BLK, HEAD_DEVS * WIDTH), jnp.bfloat16),
        in_specs=[SMEM] + [VMEM] * (2 + HEAD_DEVS),
        out_specs=VMEM,
        compiler_params=params(32),
    )(me, query_rows[0], fetched, *local)
    return mixed[None]


def solution(mesh):
    placed = (
        P("mem", "head", None),
        P("mem", "head", None),
        P("mem", "head", None),
        P("mem", None, "head"),
        P("mem", None, "head"),
        P("mem", None, None),
        P("mem", None, None),
        P("head"),
    )
    return jax.shard_map(
        on_device, mesh=mesh, in_specs=placed, out_specs=P("mem", "head", None), check_vma=False
    )
```

```python
import functools
import math

import jax
import jax.numpy as jnp
from jax import lax
from jax.experimental import pallas as pl
from jax.experimental.pallas import tpu as pltpu
from jax.sharding import Mesh
from jax.sharding import PartitionSpec as P

DH = 128
BLK = 128
HEADS_DEV = 4
CHIPS = 4
CORES = 2
HEAD_DEVS = CHIPS * CORES
PLANES = 8
MEM_DEVS = 32
PLANE_DEVS = 32
SLOTS = 8
ROWS = 32
TAIL = 16
FAR = (4, 3, 5, 2, 6)
NEAR = (0, 1, 7)
WIDTH = HEADS_DEV * DH
Q_TILE = 256
EXP_SCALE = math.log2(math.e) / math.sqrt(DH)
MASKED = -1e30


def whole(array):
    ndim = len(array.shape)
    return pl.BlockSpec(array.shape, lambda i: (0,) * ndim, pipeline_mode=pl.Buffered(1))


def call(kernel, outs, scalars, arrays, scratch=(), mib=12, hbm=()):
    outs = [pltpu.HBM(shape, jnp.bfloat16) for shape in outs]
    return pl.pallas_call(
        kernel,
        out_shape=outs,
        grid=(1,),
        in_specs=[pl.BlockSpec(memory_space=pltpu.SMEM)] * len(scalars) + [whole(a) for a in arrays],
        out_specs=[whole(o) for o in outs],
        scratch_shapes=[pltpu.VMEM(shape, jnp.bfloat16) for shape in scratch],
        compiler_params=pltpu.CompilerParams(vmem_limit_bytes=mib * 1024 * 1024),
    )(
        *scalars,
        *[
            pltpu.with_memory_space_constraint(a, pltpu.HBM) if i in hbm else a
            for i, a in enumerate(arrays)
        ],
    )


def dot_nt(a, b):
    return lax.dot_general(a, b, (((1,), (1,)), ((), ())), preferred_element_type=jnp.float32)


def spread_kernel(core_ref, keys_ref, values_ref, swapped_ref, ids_ref, out_ref):
    core = core_ref[0]
    for j in range(HEADS_DEV):
        for x in range(BLK // ROWS):
            rows, cols = pl.ds(x * ROWS, ROWS), pl.ds(j * DH, DH)
            kept = jnp.where(core == 0, keys_ref[:, rows, cols], values_ref[:, rows, cols])
            for source, piece in ((core, kept), (1 - core, swapped_ref[:, rows, cols])):
                dest = (source * HEADS_DEV + j) * (BLK // ROWS) + x
                out_ref[dest, pl.ds(0, SLOTS * ROWS), :] = piece.reshape(SLOTS * ROWS, DH)
    for dest in range(MEM_DEVS):
        out_ref[dest, pl.ds(SLOTS * ROWS, TAIL), :] = ids_ref[...]


def gather_kernel(shifts, z_ref, ids_ref, table_ref, out_ref):
    def one(dest, carry):
        for i, shift in enumerate(shifts):
            plane = (z_ref[0] + PLANES - shift) & (PLANES - 1)
            for k in range(2):
                block = ids_ref[plane * 2 * PLANE_DEVS + 2 * dest + k]
                first = pl.multiple_of((block & (SLOTS - 1)) * ROWS, ROWS)
                owner = lax.shift_right_logical(block, 3)
                out_ref[dest, 2 * i + k] = table_ref[owner, pl.ds(first, ROWS), :]
        return carry

    lax.fori_loop(0, PLANE_DEVS, one, 0, unroll=4)


def query_kernel(z_ref, q_ref, *out_refs):
    for shift in range(PLANES):
        plane = (z_ref[0] + shift) % PLANES
        for y in range(HEADS_DEV):
            cols = pl.ds(pl.multiple_of((y * PLANES + plane) * DH, DH), DH)
            out_refs[shift][y] = q_ref[:, cols]


def attend_kernel(count, *refs):
    queries, fetched_ref, outs = refs[:count], refs[count], refs[count + 1 :]
    for i in range(count):
        for y in range(HEADS_DEV):
            keys = fetched_ref[:, y, 0, pl.ds(2 * i, 2)].reshape(2 * BLK, DH)
            values = fetched_ref[:, y, 1, pl.ds(2 * i, 2)].reshape(2 * BLK, DH)
            scores = dot_nt(queries[i][y], keys)
            top = jnp.max(scores, axis=1, keepdims=True)
            weights = jnp.exp2((scores - top) * EXP_SCALE)
            total = jnp.sum(weights, axis=1, keepdims=True)
            part = jnp.dot(weights.astype(jnp.bfloat16), values, preferred_element_type=jnp.float32)
            outs[i][y] = (part / total).astype(jnp.bfloat16)


def pack_kernel(me_ref, q_ref, k_ref, v_ref, *out_refs):
    for shift in range(HEAD_DEVS):
        dest = (me_ref[0] + shift) % HEAD_DEVS
        cols = pl.ds(pl.multiple_of(dest * WIDTH, WIDTH), WIDTH)
        for i, ref in enumerate((q_ref, k_ref, v_ref)):
            out_refs[shift][i] = ref[:, cols]


def local_kernel(me_ref, gate_ref, *refs):
    ins, outs = refs[:HEAD_DEVS], refs[HEAD_DEVS : HEAD_DEVS + CORES]
    held, result = refs[HEAD_DEVS + CORES :]
    me = me_ref[0]
    for shift in range(HEAD_DEVS):
        held[:, (me + HEAD_DEVS - shift) % HEAD_DEVS] = ins[shift][...]
    length = HEAD_DEVS * BLK
    blocks = Q_TILE // BLK
    parts = []
    for j in range(HEADS_DEV):
        cols = pl.ds(j * DH, DH)
        gate = jax.nn.sigmoid(jnp.full((1, DH), gate_ref[j], jnp.float32))
        high = gate.astype(jnp.bfloat16)
        rest = gate - high.astype(jnp.float32)
        mid = rest.astype(jnp.bfloat16)
        low = (rest - mid.astype(jnp.float32)).astype(jnp.bfloat16)
        parts.append((high, mid, low))
        for tile in range(length // Q_TILE):
            rows = pl.ds(tile * blocks, blocks)
            query = held[0, rows, :, cols].reshape(Q_TILE, DH)
            diag = dot_nt(query, held[1, rows, :, cols].reshape(Q_TILE, DH))
            row_ids = lax.broadcasted_iota(jnp.int32, (Q_TILE, Q_TILE), 0)
            col_ids = lax.broadcasted_iota(jnp.int32, (Q_TILE, Q_TILE), 1)
            diag = jnp.where(col_ids <= row_ids, diag, MASKED)
            top = jnp.max(diag, axis=1, keepdims=True)
            if tile:
                before = pl.ds(0, tile * blocks)
                off = dot_nt(query, held[1, before, :, cols].reshape(tile * Q_TILE, DH))
                top = jnp.maximum(top, jnp.max(off, axis=1, keepdims=True))
            weights = jnp.exp2((diag - top) * EXP_SCALE)
            total = jnp.sum(weights, axis=1, keepdims=True)
            part = jnp.dot(
                weights.astype(jnp.bfloat16),
                held[2, rows, :, cols].reshape(Q_TILE, DH),
                preferred_element_type=jnp.float32,
            )
            if tile:
                weights = jnp.exp2((off - top) * EXP_SCALE)
                total = total + jnp.sum(weights, axis=1, keepdims=True)
                part = part + jnp.dot(
                    weights.astype(jnp.bfloat16),
                    held[2, before, :, cols].reshape(tile * Q_TILE, DH),
                    preferred_element_type=jnp.float32,
                )
            part = part * ((1.0 - gate) / total)
            result[rows, j] = part.astype(jnp.bfloat16).reshape(blocks, BLK, DH)
    for i, out in enumerate(outs):
        for chip in range(CHIPS):
            out[chip, :, pl.ds(0, BLK), :] = result[chip * CORES + (me + i) % CORES]
            for j in range(HEADS_DEV):
                filler = jnp.zeros((TAIL - 3, DH), jnp.bfloat16)
                rows = jnp.concatenate([*parts[j], filler], axis=0)
                out[chip, j, pl.ds(BLK, TAIL), :] = rows


def merge_kernel(me_ref, own_ref, other_ref, *out_refs):
    core = me_ref[0] % CORES
    for shift in range(CHIPS):
        chip = (me_ref[0] // CORES + shift) % CHIPS
        out_refs[shift][core] = own_ref[chip]
        out_refs[shift][1 - core] = other_ref[chip]


def mix_kernel(me_ref, z_ref, *refs):
    memory, local = refs[:PLANES], refs[PLANES : PLANES + CHIPS]
    out_ref, held = refs[PLANES + CHIPS :]
    for shift in range(CHIPS):
        chip = (me_ref[0] // CORES + CHIPS - shift) % CHIPS
        for core in range(CORES):
            first = (chip * CORES + core) * HEADS_DEV
            held[pl.ds(first, HEADS_DEV)] = local[shift][core]
    for shift in range(PLANES):
        plane = (z_ref[0] + shift) % PLANES
        for y in range(HEADS_DEV):
            head = y * PLANES + plane
            gate = held[head, pl.ds(BLK, TAIL), :].astype(jnp.float32)
            gate = gate[0:1] + gate[1:2] + gate[2:3]
            part = memory[shift][y].astype(jnp.float32) * gate
            part = part + held[head, pl.ds(0, BLK), :].astype(jnp.float32)
            out_ref[:, pl.ds(pl.multiple_of(head * DH, DH), DH)] = part.astype(jnp.bfloat16)


def shifted(array, axis, size, shift):
    if shift % size == 0:
        return array
    return lax.ppermute(array, axis, [(i, (i + shift) % size) for i in range(size)])


def on_device(
    query_rows, key_rows, value_rows, memory_keys, memory_values, owner_list, slot_list, gate_logit
):
    core = lax.axis_index("c")
    z = lax.axis_index("z").astype(jnp.int32).reshape(1)
    me = lax.axis_index(("y", "c")).astype(jnp.int32).reshape(1)
    query = query_rows[0]

    swapped = shifted(jnp.where(core == 0, memory_values, memory_keys), "c", CORES, 1)
    ids = (owner_list * SLOTS + slot_list).reshape(TAIL, 1)
    ids = jnp.broadcast_to(ids.astype(jnp.bfloat16), (TAIL, DH))
    (spread,) = call(
        spread_kernel,
        [(MEM_DEVS, SLOTS * ROWS + TAIL, DH)],
        [core.astype(jnp.int32).reshape(1)],
        [memory_keys, memory_values, swapped, ids],
    )
    table = lax.all_to_all(spread, ("z", "x"), split_axis=0, concat_axis=0, tiled=True)

    packed = call(
        pack_kernel, [(3, BLK, WIDTH)] * HEAD_DEVS, [me], [query, key_rows[0], value_rows[0]]
    )
    packed = [shifted(packed[s], ("y", "c"), HEAD_DEVS, s) for s in range(HEAD_DEVS)]
    local = call(
        local_kernel,
        [(CHIPS, HEADS_DEV, BLK + TAIL, DH)] * CORES,
        [me, gate_logit],
        packed,
        [(3, HEAD_DEVS, BLK, WIDTH), (HEAD_DEVS, HEADS_DEV, BLK, DH)],
        24,
        range(HEAD_DEVS),
    )
    table, local = lax.optimization_barrier((table, local))

    all_ids = table[:, SLOTS * ROWS :, 0].astype(jnp.int32).reshape(MEM_DEVS * TAIL)

    def gathered(shifts, table):
        return call(
            functools.partial(gather_kernel, shifts),
            [(PLANE_DEVS, 2 * len(shifts), ROWS, DH)],
            [z, all_ids],
            [table],
        )[0]

    def fetch(requested):
        fetched = lax.all_to_all(
            requested, ("x", "y", "c"), split_axis=0, concat_axis=0, tiled=True
        )
        return fetched.reshape(BLK // ROWS, HEADS_DEV, 2, -1, ROWS, DH)

    def attend(shifts, fetched):
        return call(
            functools.partial(attend_kernel, len(shifts)),
            [(HEADS_DEV, BLK, DH)] * len(shifts),
            [],
            [asked[s] for s in shifts] + [fetched],
            hbm=range(len(shifts)),
        )

    far, table, query, local = lax.optimization_barrier((gathered(FAR, table), table, query, local))
    far = fetch(far)
    near = gathered(NEAR, table)
    local = [local[0], shifted(local[1], "c", CORES, 1)]
    local = call(merge_kernel, [(CORES, HEADS_DEV, BLK + TAIL, DH)] * CHIPS, [me], local)
    asked = call(query_kernel, [(HEADS_DEV, BLK, DH)] * PLANES, [z], [query])
    asked = [shifted(asked[s], "z", PLANES, s) for s in range(PLANES)]
    far, near, asked, local = lax.optimization_barrier((far, near, asked, local))

    near = fetch(near)
    memory = {s: shifted(part, "z", PLANES, -s) for s, part in zip(FAR, attend(FAR, far))}
    memory[6], local = lax.optimization_barrier((memory[6], local))
    local = [shifted(local[s], "y", CHIPS, s) for s in range(CHIPS)]
    memory.update({s: shifted(part, "z", PLANES, -s) for s, part in zip(NEAR, attend(NEAR, near))})

    (mixed,) = call(
        mix_kernel,
        [(BLK, HEAD_DEVS * WIDTH)],
        [me, z],
        [memory[s] for s in range(PLANES)] + local,
        [(HEAD_DEVS * HEADS_DEV, BLK + TAIL, DH)],
        hbm=range(PLANES + CHIPS),
    )
    return mixed[None]


def solution(mesh):
    fine = Mesh(mesh.devices.reshape(8, 4, 4, 2), ("z", "x", "y", "c"))
    mem, head = ("z", "x"), ("y", "c")
    placed = (
        P(mem, head, None),
        P(mem, head, None),
        P(mem, head, None),
        P(mem, None, head),
        P(mem, None, head),
        P(mem, None, None),
        P(mem, None, None),
        P(head),
    )
    return jax.shard_map(
        on_device, mesh=fine, in_specs=placed, out_specs=P(mem, head, None), check_vma=False
    )
```

```python
import functools
import math

import jax
import jax.numpy as jnp
from jax import lax
from jax.experimental import pallas as pl
from jax.experimental.pallas import tpu as pltpu
from jax.sharding import Mesh
from jax.sharding import PartitionSpec as P

DH = 128
BLK = 128
HEADS_DEV = 4
CHIPS = 4
CORES = 2
HEAD_DEVS = CHIPS * CORES
PLANES = 8
MEM_DEVS = 32
PLANE_DEVS = 32
SLOTS = 8
ROWS = 32
TAIL = 16
FAR = (4, 3, 5, 2, 6)
NEAR = (0, 1, 7)
WIDTH = HEADS_DEV * DH
Q_TILE = 256
EXP_SCALE = math.log2(math.e) / math.sqrt(DH)
MASKED = -1e30


def whole(array):
    ndim = len(array.shape)
    return pl.BlockSpec(array.shape, lambda i: (0,) * ndim, pipeline_mode=pl.Buffered(1))


def call(kernel, outs, scalars, arrays, scratch=(), mib=12, hbm=()):
    outs = [pltpu.HBM(shape, jnp.bfloat16) for shape in outs]
    return pl.pallas_call(
        kernel,
        out_shape=outs,
        grid=(1,),
        in_specs=[pl.BlockSpec(memory_space=pltpu.SMEM)] * len(scalars) + [whole(a) for a in arrays],
        out_specs=[whole(o) for o in outs],
        scratch_shapes=[pltpu.VMEM(shape, jnp.bfloat16) for shape in scratch],
        compiler_params=pltpu.CompilerParams(vmem_limit_bytes=mib * 1024 * 1024),
    )(
        *scalars,
        *[
            pltpu.with_memory_space_constraint(a, pltpu.HBM) if i in hbm else a
            for i, a in enumerate(arrays)
        ],
    )


def dot_nt(a, b):
    return lax.dot_general(a, b, (((1,), (1,)), ((), ())), preferred_element_type=jnp.float32)


def spread_kernel(core_ref, keys_ref, swapped_ref, ids_ref, out_ref):
    core = core_ref[0]
    for source, ref in ((core, keys_ref), (1 - core, swapped_ref)):
        for j in range(HEADS_DEV):
            for x in range(BLK // ROWS):
                dest = (source * HEADS_DEV + j) * (BLK // ROWS) + x
                piece = ref[:, pl.ds(x * ROWS, ROWS), pl.ds(j * DH, DH)]
                out_ref[dest, pl.ds(0, SLOTS * ROWS), :] = piece.reshape(SLOTS * ROWS, DH)
    for dest in range(MEM_DEVS):
        out_ref[dest, pl.ds(SLOTS * ROWS, TAIL), :] = ids_ref[...]


def gather_kernel(shifts, z_ref, ids_ref, table_ref, out_ref):
    def one(dest, carry):
        for i, shift in enumerate(shifts):
            plane = (z_ref[0] + PLANES - shift) & (PLANES - 1)
            for k in range(2):
                block = ids_ref[plane * 2 * PLANE_DEVS + 2 * dest + k]
                first = pl.multiple_of((block & (SLOTS - 1)) * ROWS, ROWS)
                owner = lax.shift_right_logical(block, 3)
                out_ref[dest, 2 * i + k] = table_ref[owner, pl.ds(first, ROWS), :]
        return carry

    lax.fori_loop(0, PLANE_DEVS, one, 0, unroll=4)


def query_kernel(z_ref, q_ref, *out_refs):
    for shift in range(PLANES):
        plane = (z_ref[0] + shift) % PLANES
        for y in range(HEADS_DEV):
            cols = pl.ds(pl.multiple_of((y * PLANES + plane) * DH, DH), DH)
            out_refs[shift][y] = q_ref[:, cols]


def attend_kernel(count, z_ref, *refs):
    core = z_ref[0] // HEADS_DEV
    queries, fetched_ref, outs = refs[:count], refs[count], refs[count + 1 :]
    for i in range(count):
        for y in range(HEADS_DEV):
            keys = fetched_ref[:, y, core, pl.ds(2 * i, 2)].reshape(2 * BLK, DH)
            values = fetched_ref[:, y, 1 - core, pl.ds(2 * i, 2)].reshape(2 * BLK, DH)
            scores = dot_nt(queries[i][y], keys)
            top = jnp.max(scores, axis=1, keepdims=True)
            weights = jnp.exp2((scores - top) * EXP_SCALE)
            total = jnp.sum(weights, axis=1, keepdims=True)
            part = jnp.dot(weights.astype(jnp.bfloat16), values, preferred_element_type=jnp.float32)
            outs[i][y] = (part / total).astype(jnp.bfloat16)


def pack_kernel(me_ref, q_ref, k_ref, v_ref, *out_refs):
    for shift in range(HEAD_DEVS):
        dest = (me_ref[0] + shift) % HEAD_DEVS
        cols = pl.ds(pl.multiple_of(dest * WIDTH, WIDTH), WIDTH)
        for i, ref in enumerate((q_ref, k_ref, v_ref)):
            out_refs[shift][i] = ref[:, cols]


def local_kernel(me_ref, gate_ref, *refs):
    ins, outs = refs[:HEAD_DEVS], refs[HEAD_DEVS : HEAD_DEVS + CORES]
    held, result = refs[HEAD_DEVS + CORES :]
    me = me_ref[0]
    for shift in range(HEAD_DEVS):
        held[:, (me + HEAD_DEVS - shift) % HEAD_DEVS] = ins[shift][...]
    length = HEAD_DEVS * BLK
    blocks = Q_TILE // BLK
    parts = []
    for j in range(HEADS_DEV):
        cols = pl.ds(j * DH, DH)
        gate = jax.nn.sigmoid(jnp.full((1, DH), gate_ref[j], jnp.float32))
        high = gate.astype(jnp.bfloat16)
        rest = gate - high.astype(jnp.float32)
        mid = rest.astype(jnp.bfloat16)
        low = (rest - mid.astype(jnp.float32)).astype(jnp.bfloat16)
        parts.append((high, mid, low))
        for tile in range(length // Q_TILE):
            rows = pl.ds(tile * blocks, blocks)
            query = held[0, rows, :, cols].reshape(Q_TILE, DH)
            diag = dot_nt(query, held[1, rows, :, cols].reshape(Q_TILE, DH))
            row_ids = lax.broadcasted_iota(jnp.int32, (Q_TILE, Q_TILE), 0)
            col_ids = lax.broadcasted_iota(jnp.int32, (Q_TILE, Q_TILE), 1)
            diag = jnp.where(col_ids <= row_ids, diag, MASKED)
            top = jnp.max(diag, axis=1, keepdims=True)
            if tile:
                before = pl.ds(0, tile * blocks)
                off = dot_nt(query, held[1, before, :, cols].reshape(tile * Q_TILE, DH))
                top = jnp.maximum(top, jnp.max(off, axis=1, keepdims=True))
            weights = jnp.exp2((diag - top) * EXP_SCALE)
            total = jnp.sum(weights, axis=1, keepdims=True)
            part = jnp.dot(
                weights.astype(jnp.bfloat16),
                held[2, rows, :, cols].reshape(Q_TILE, DH),
                preferred_element_type=jnp.float32,
            )
            if tile:
                weights = jnp.exp2((off - top) * EXP_SCALE)
                total = total + jnp.sum(weights, axis=1, keepdims=True)
                part = part + jnp.dot(
                    weights.astype(jnp.bfloat16),
                    held[2, before, :, cols].reshape(tile * Q_TILE, DH),
                    preferred_element_type=jnp.float32,
                )
            part = part * ((1.0 - gate) / total)
            result[rows, j] = part.astype(jnp.bfloat16).reshape(blocks, BLK, DH)
    for i, out in enumerate(outs):
        for chip in range(CHIPS):
            out[chip, :, pl.ds(0, BLK), :] = result[chip * CORES + (me + i) % CORES]
            for j in range(HEADS_DEV):
                filler = jnp.zeros((TAIL - 3, DH), jnp.bfloat16)
                rows = jnp.concatenate([*parts[j], filler], axis=0)
                out[chip, j, pl.ds(BLK, TAIL), :] = rows


def merge_kernel(me_ref, own_ref, other_ref, *out_refs):
    core = me_ref[0] % CORES
    for shift in range(CHIPS):
        chip = (me_ref[0] // CORES + shift) % CHIPS
        out_refs[shift][core] = own_ref[chip]
        out_refs[shift][1 - core] = other_ref[chip]


def mix_kernel(me_ref, z_ref, *refs):
    memory, local = refs[:PLANES], refs[PLANES : PLANES + CHIPS]
    out_ref, held = refs[PLANES + CHIPS :]
    for shift in range(CHIPS):
        chip = (me_ref[0] // CORES + CHIPS - shift) % CHIPS
        for core in range(CORES):
            first = (chip * CORES + core) * HEADS_DEV
            held[pl.ds(first, HEADS_DEV)] = local[shift][core]
    for shift in range(PLANES):
        plane = (z_ref[0] + shift) % PLANES
        for y in range(HEADS_DEV):
            head = y * PLANES + plane
            gate = held[head, pl.ds(BLK, TAIL), :].astype(jnp.float32)
            gate = gate[0:1] + gate[1:2] + gate[2:3]
            part = memory[shift][y].astype(jnp.float32) * gate
            part = part + held[head, pl.ds(0, BLK), :].astype(jnp.float32)
            out_ref[:, pl.ds(pl.multiple_of(head * DH, DH), DH)] = part.astype(jnp.bfloat16)


def shifted(array, axis, size, shift):
    if shift % size == 0:
        return array
    return lax.ppermute(array, axis, [(i, (i + shift) % size) for i in range(size)])


def on_device(
    query_rows, key_rows, value_rows, memory_keys, memory_values, owner_list, slot_list, gate_logit
):
    core = lax.axis_index("c")
    z = lax.axis_index("z").astype(jnp.int32).reshape(1)
    me = lax.axis_index(("y", "c")).astype(jnp.int32).reshape(1)
    query = query_rows[0]

    swapped = shifted(memory_values, "c", CORES, 1)
    ids = (owner_list * SLOTS + slot_list).reshape(TAIL, 1)
    ids = jnp.broadcast_to(ids.astype(jnp.bfloat16), (TAIL, DH))
    (spread,) = call(
        spread_kernel,
        [(MEM_DEVS, SLOTS * ROWS + TAIL, DH)],
        [core.astype(jnp.int32).reshape(1)],
        [memory_keys, swapped, ids],
    )
    table = lax.all_to_all(spread, ("z", "x"), split_axis=0, concat_axis=0, tiled=True)

    packed = call(
        pack_kernel, [(3, BLK, WIDTH)] * HEAD_DEVS, [me], [query, key_rows[0], value_rows[0]]
    )
    packed = [shifted(packed[s], ("y", "c"), HEAD_DEVS, s) for s in range(HEAD_DEVS)]
    local = call(
        local_kernel,
        [(CHIPS, HEADS_DEV, BLK + TAIL, DH)] * CORES,
        [me, gate_logit],
        packed,
        [(3, HEAD_DEVS, BLK, WIDTH), (HEAD_DEVS, HEADS_DEV, BLK, DH)],
        24,
        range(HEAD_DEVS),
    )
    asked = call(query_kernel, [(HEADS_DEV, BLK, DH)] * PLANES, [z], [query])
    table, local, asked = lax.optimization_barrier((table, local, asked))

    all_ids = table[:, SLOTS * ROWS :, 0].astype(jnp.int32).reshape(MEM_DEVS * TAIL)

    def gathered(shifts, table):
        return call(
            functools.partial(gather_kernel, shifts),
            [(PLANE_DEVS, 2 * len(shifts), ROWS, DH)],
            [z, all_ids],
            [table],
        )[0]

    def fetch(requested):
        fetched = lax.all_to_all(
            requested, ("x", "y", "c"), split_axis=0, concat_axis=0, tiled=True
        )
        return fetched.reshape(BLK // ROWS, HEADS_DEV, 2, -1, ROWS, DH)

    def attend(shifts, fetched):
        return call(
            functools.partial(attend_kernel, len(shifts)),
            [(HEADS_DEV, BLK, DH)] * len(shifts),
            [z],
            [asked[s] for s in shifts] + [fetched],
            hbm=range(len(shifts)),
        )

    far, table, asked, local = lax.optimization_barrier((gathered(FAR, table), table, asked, local))
    far = fetch(far)
    near = gathered(NEAR, table)
    local = [local[0], shifted(local[1], "c", CORES, 1)]
    local = call(merge_kernel, [(CORES, HEADS_DEV, BLK + TAIL, DH)] * CHIPS, [me], local)
    asked = {s: shifted(asked[s], "z", PLANES, s) for s in FAR + NEAR}
    far, near, asked, local = lax.optimization_barrier((far, near, asked, local))

    parts, near = lax.optimization_barrier((attend(FAR, far), near))
    near = fetch(near)
    memory = {s: shifted(part, "z", PLANES, -s) for s, part in zip(FAR, parts)}
    memory[6], local = lax.optimization_barrier((memory[6], local))
    local = [shifted(local[s], "y", CHIPS, s) for s in range(CHIPS)]
    memory.update({s: shifted(part, "z", PLANES, -s) for s, part in zip(NEAR, attend(NEAR, near))})

    (mixed,) = call(
        mix_kernel,
        [(BLK, HEAD_DEVS * WIDTH)],
        [me, z],
        [memory[s] for s in range(PLANES)] + local,
        [(HEAD_DEVS * HEADS_DEV, BLK + TAIL, DH)],
        hbm=range(PLANES + CHIPS),
    )
    return mixed[None]


def solution(mesh):
    fine = Mesh(mesh.devices.reshape(8, 4, 4, 2), ("z", "x", "y", "c"))
    mem, head = ("z", "x"), ("y", "c")
    placed = (
        P(mem, head, None),
        P(mem, head, None),
        P(mem, head, None),
        P(mem, None, head),
        P(mem, None, head),
        P(mem, None, None),
        P(mem, None, None),
        P(head),
    )
    return jax.shard_map(
        on_device, mesh=fine, in_specs=placed, out_specs=P(mem, head, None), check_vma=False
    )
```

```python
import functools
import math

import jax
import jax.numpy as jnp
from jax import lax
from jax.experimental import pallas as pl
from jax.experimental.pallas import tpu as pltpu
from jax.sharding import Mesh
from jax.sharding import PartitionSpec as P

DH = 128
BLK = 128
HEADS_DEV = 4
CHIPS = 4
CORES = 2
HEAD_DEVS = CHIPS * CORES
PLANES = 8
MEM_DEVS = 32
PLANE_DEVS = 32
SLOTS = 8
ROWS = 32
TAIL = 16
FAR = (4, 3, 5, 2, 6)
NEAR = (0, 1, 7)
WIDTH = HEADS_DEV * DH
Q_TILE = 256
EXP_SCALE = math.log2(math.e) / math.sqrt(DH)
MASKED = -1e30


def whole(array):
    ndim = len(array.shape)
    return pl.BlockSpec(array.shape, lambda i: (0,) * ndim, pipeline_mode=pl.Buffered(1))


def call(kernel, outs, scalars, arrays, scratch=(), mib=12, hbm=()):
    outs = [pltpu.HBM(shape, jnp.bfloat16) for shape in outs]
    return pl.pallas_call(
        kernel,
        out_shape=outs,
        grid=(1,),
        in_specs=[pl.BlockSpec(memory_space=pltpu.SMEM)] * len(scalars) + [whole(a) for a in arrays],
        out_specs=[whole(o) for o in outs],
        scratch_shapes=[pltpu.VMEM(shape, jnp.bfloat16) for shape in scratch],
        compiler_params=pltpu.CompilerParams(vmem_limit_bytes=mib * 1024 * 1024),
    )(
        *scalars,
        *[
            pltpu.with_memory_space_constraint(a, pltpu.HBM) if i in hbm else a
            for i, a in enumerate(arrays)
        ],
    )


def dot_nt(a, b):
    return lax.dot_general(a, b, (((1,), (1,)), ((), ())), preferred_element_type=jnp.float32)


def spread_kernel(core_ref, keys_ref, swapped_ref, ids_ref, out_ref):
    core = core_ref[0]
    for source, ref in ((core, keys_ref), (1 - core, swapped_ref)):
        for j in range(HEADS_DEV):
            for x in range(BLK // ROWS):
                dest = (source * HEADS_DEV + j) * (BLK // ROWS) + x
                piece = ref[:, pl.ds(x * ROWS, ROWS), pl.ds(j * DH, DH)]
                out_ref[dest, pl.ds(0, SLOTS * ROWS), :] = piece.reshape(SLOTS * ROWS, DH)
    for dest in range(MEM_DEVS):
        out_ref[dest, pl.ds(SLOTS * ROWS, TAIL), :] = ids_ref[...]


def gather_kernel(shifts, z_ref, ids_ref, table_ref, out_ref):
    start = pl.program_id(0) * out_ref.shape[0]

    def one(row, carry):
        dest = start + row
        for i, shift in enumerate(shifts):
            plane = (z_ref[0] + PLANES - shift) & (PLANES - 1)
            for k in range(2):
                block = ids_ref[plane * 2 * PLANE_DEVS + 2 * dest + k]
                first = pl.multiple_of((block & (SLOTS - 1)) * ROWS, ROWS)
                owner = lax.shift_right_logical(block, 3)
                out_ref[row, 2 * i + k] = table_ref[owner, pl.ds(first, ROWS), :]
        return carry

    lax.fori_loop(0, out_ref.shape[0], one, 0, unroll=4)


def query_kernel(z_ref, q_ref, *out_refs):
    for shift in range(PLANES):
        plane = (z_ref[0] + shift) % PLANES
        for y in range(HEADS_DEV):
            cols = pl.ds(pl.multiple_of((y * PLANES + plane) * DH, DH), DH)
            out_refs[shift][y] = q_ref[:, cols]


def attend_kernel(count, z_ref, *refs):
    core = z_ref[0] // HEADS_DEV
    queries, fetched_ref, outs = refs[:count], refs[count], refs[count + 1 :]
    for i in range(count):
        for y in range(HEADS_DEV):
            keys = fetched_ref[:, y, core, pl.ds(2 * i, 2)].reshape(2 * BLK, DH)
            values = fetched_ref[:, y, 1 - core, pl.ds(2 * i, 2)].reshape(2 * BLK, DH)
            scores = dot_nt(queries[i][y], keys)
            top = jnp.max(scores, axis=1, keepdims=True)
            weights = jnp.exp2((scores - top) * EXP_SCALE)
            total = jnp.sum(weights, axis=1, keepdims=True)
            part = jnp.dot(weights.astype(jnp.bfloat16), values, preferred_element_type=jnp.float32)
            outs[i][y] = (part / total).astype(jnp.bfloat16)


def pack_kernel(me_ref, q_ref, k_ref, v_ref, *out_refs):
    for shift in range(HEAD_DEVS):
        dest = (me_ref[0] + shift) % HEAD_DEVS
        cols = pl.ds(pl.multiple_of(dest * WIDTH, WIDTH), WIDTH)
        for i, ref in enumerate((q_ref, k_ref, v_ref)):
            out_refs[shift][i] = ref[:, cols]


def local_kernel(me_ref, gate_ref, *refs):
    ins, outs = refs[:HEAD_DEVS], refs[HEAD_DEVS : HEAD_DEVS + CORES]
    held, result = refs[HEAD_DEVS + CORES :]
    me = me_ref[0]
    for shift in range(HEAD_DEVS):
        held[:, (me + HEAD_DEVS - shift) % HEAD_DEVS] = ins[shift][...]
    length = HEAD_DEVS * BLK
    blocks = Q_TILE // BLK
    parts = []
    for j in range(HEADS_DEV):
        cols = pl.ds(j * DH, DH)
        gate = jax.nn.sigmoid(jnp.full((1, DH), gate_ref[j], jnp.float32))
        high = gate.astype(jnp.bfloat16)
        rest = gate - high.astype(jnp.float32)
        mid = rest.astype(jnp.bfloat16)
        low = (rest - mid.astype(jnp.float32)).astype(jnp.bfloat16)
        parts.append((high, mid, low))
        for tile in range(length // Q_TILE):
            rows = pl.ds(tile * blocks, blocks)
            query = held[0, rows, :, cols].reshape(Q_TILE, DH)
            diag = dot_nt(query, held[1, rows, :, cols].reshape(Q_TILE, DH))
            row_ids = lax.broadcasted_iota(jnp.int32, (Q_TILE, Q_TILE), 0)
            col_ids = lax.broadcasted_iota(jnp.int32, (Q_TILE, Q_TILE), 1)
            diag = jnp.where(col_ids <= row_ids, diag, MASKED)
            top = jnp.max(diag, axis=1, keepdims=True)
            if tile:
                before = pl.ds(0, tile * blocks)
                off = dot_nt(query, held[1, before, :, cols].reshape(tile * Q_TILE, DH))
                top = jnp.maximum(top, jnp.max(off, axis=1, keepdims=True))
            weights = jnp.exp2((diag - top) * EXP_SCALE)
            total = jnp.sum(weights, axis=1, keepdims=True)
            part = jnp.dot(
                weights.astype(jnp.bfloat16),
                held[2, rows, :, cols].reshape(Q_TILE, DH),
                preferred_element_type=jnp.float32,
            )
            if tile:
                weights = jnp.exp2((off - top) * EXP_SCALE)
                total = total + jnp.sum(weights, axis=1, keepdims=True)
                part = part + jnp.dot(
                    weights.astype(jnp.bfloat16),
                    held[2, before, :, cols].reshape(tile * Q_TILE, DH),
                    preferred_element_type=jnp.float32,
                )
            part = part * ((1.0 - gate) / total)
            result[rows, j] = part.astype(jnp.bfloat16).reshape(blocks, BLK, DH)
    for i, out in enumerate(outs):
        for chip in range(CHIPS):
            out[chip, :, pl.ds(0, BLK), :] = result[chip * CORES + (me + i) % CORES]
            for j in range(HEADS_DEV):
                filler = jnp.zeros((TAIL - 3, DH), jnp.bfloat16)
                rows = jnp.concatenate([*parts[j], filler], axis=0)
                out[chip, j, pl.ds(BLK, TAIL), :] = rows


def merge_kernel(me_ref, own_ref, other_ref, *out_refs):
    core = me_ref[0] % CORES
    for shift in range(CHIPS):
        chip = (me_ref[0] // CORES + shift) % CHIPS
        out_refs[shift][core] = own_ref[chip]
        out_refs[shift][1 - core] = other_ref[chip]


def mix_kernel(me_ref, z_ref, *refs):
    memory, local = refs[:PLANES], refs[PLANES : PLANES + CHIPS]
    out_ref, held = refs[PLANES + CHIPS :]
    for shift in range(CHIPS):
        chip = (me_ref[0] // CORES + CHIPS - shift) % CHIPS
        for core in range(CORES):
            first = (chip * CORES + core) * HEADS_DEV
            held[pl.ds(first, HEADS_DEV)] = local[shift][core]
    for shift in range(PLANES):
        plane = (z_ref[0] + shift) % PLANES
        for y in range(HEADS_DEV):
            head = y * PLANES + plane
            gate = held[head, pl.ds(BLK, TAIL), :].astype(jnp.float32)
            gate = gate[0:1] + gate[1:2] + gate[2:3]
            part = memory[shift][y].astype(jnp.float32) * gate
            part = part + held[head, pl.ds(0, BLK), :].astype(jnp.float32)
            out_ref[:, pl.ds(pl.multiple_of(head * DH, DH), DH)] = part.astype(jnp.bfloat16)


def shifted(array, axis, size, shift):
    if shift % size == 0:
        return array
    return lax.ppermute(array, axis, [(i, (i + shift) % size) for i in range(size)])


def on_device(
    query_rows, key_rows, value_rows, memory_keys, memory_values, owner_list, slot_list, gate_logit
):
    core = lax.axis_index("c")
    z = lax.axis_index("z").astype(jnp.int32).reshape(1)
    me = lax.axis_index(("y", "c")).astype(jnp.int32).reshape(1)
    query = query_rows[0]

    swapped = shifted(memory_values, "c", CORES, 1)
    ids = (owner_list * SLOTS + slot_list).reshape(TAIL, 1)
    ids = jnp.broadcast_to(ids.astype(jnp.bfloat16), (TAIL, DH))
    (spread,) = call(
        spread_kernel,
        [(MEM_DEVS, SLOTS * ROWS + TAIL, DH)],
        [core.astype(jnp.int32).reshape(1)],
        [memory_keys, swapped, ids],
    )
    table = lax.all_to_all(spread, ("z", "x"), split_axis=0, concat_axis=0, tiled=True)

    packed = call(
        pack_kernel, [(3, BLK, WIDTH)] * HEAD_DEVS, [me], [query, key_rows[0], value_rows[0]]
    )
    packed = [shifted(packed[s], ("y", "c"), HEAD_DEVS, s) for s in range(HEAD_DEVS)]
    local = call(
        local_kernel,
        [(CHIPS, HEADS_DEV, BLK + TAIL, DH)] * CORES,
        [me, gate_logit],
        packed,
        [(3, HEAD_DEVS, BLK, WIDTH), (HEAD_DEVS, HEADS_DEV, BLK, DH)],
        24,
        range(HEAD_DEVS),
    )
    asked = call(query_kernel, [(HEADS_DEV, BLK, DH)] * PLANES, [z], [query])
    table, local, asked = lax.optimization_barrier((table, local, asked))

    all_ids = table[:, SLOTS * ROWS :, 0].astype(jnp.int32).reshape(MEM_DEVS * TAIL)

    def gathered(shifts, table):
        shape = (PLANE_DEVS, 2 * len(shifts), ROWS, DH)
        smem = pl.BlockSpec(memory_space=pltpu.SMEM)
        return pl.pallas_call(
            functools.partial(gather_kernel, shifts),
            out_shape=pltpu.HBM(shape, jnp.bfloat16),
            grid=(4,),
            in_specs=[smem, smem, whole(table)],
            out_specs=pl.BlockSpec((PLANE_DEVS // 4, *shape[1:]), lambda i: (i, 0, 0, 0)),
            compiler_params=pltpu.CompilerParams(vmem_limit_bytes=12 * 1024 * 1024),
        )(z, all_ids, table)

    def fetch(requested):
        fetched = lax.all_to_all(
            requested, ("x", "y", "c"), split_axis=0, concat_axis=0, tiled=True
        )
        return fetched.reshape(BLK // ROWS, HEADS_DEV, 2, -1, ROWS, DH)

    def attend(shifts, fetched):
        return call(
            functools.partial(attend_kernel, len(shifts)),
            [(HEADS_DEV, BLK, DH)] * len(shifts),
            [z],
            [asked[s] for s in shifts] + [fetched],
            hbm=range(len(shifts)),
        )

    far, table, asked, local = lax.optimization_barrier((gathered(FAR, table), table, asked, local))
    far = fetch(far)
    near = gathered(NEAR, table)
    local = [local[0], shifted(local[1], "c", CORES, 1)]
    local = call(merge_kernel, [(CORES, HEADS_DEV, BLK + TAIL, DH)] * CHIPS, [me], local)
    asked = {s: shifted(asked[s], "z", PLANES, s) for s in FAR + NEAR}
    far, near, asked, local = lax.optimization_barrier((far, near, asked, local))

    parts, near = lax.optimization_barrier((attend(FAR, far), near))
    near = fetch(near)
    memory = {s: shifted(part, "z", PLANES, -s) for s, part in zip(FAR, parts)}
    memory[6], local = lax.optimization_barrier((memory[6], local))
    local = [shifted(local[s], "y", CHIPS, s) for s in range(CHIPS)]
    memory.update({s: shifted(part, "z", PLANES, -s) for s, part in zip(NEAR, attend(NEAR, near))})

    (mixed,) = call(
        mix_kernel,
        [(BLK, HEAD_DEVS * WIDTH)],
        [me, z],
        [memory[s] for s in range(PLANES)] + local,
        [(HEAD_DEVS * HEADS_DEV, BLK + TAIL, DH)],
        hbm=range(PLANES + CHIPS),
    )
    return mixed[None]


def solution(mesh):
    fine = Mesh(mesh.devices.reshape(8, 4, 4, 2), ("z", "x", "y", "c"))
    mem, head = ("z", "x"), ("y", "c")
    placed = (
        P(mem, head, None),
        P(mem, head, None),
        P(mem, head, None),
        P(mem, None, head),
        P(mem, None, head),
        P(mem, None, None),
        P(mem, None, None),
        P(head),
    )
    return jax.shard_map(
        on_device, mesh=fine, in_specs=placed, out_specs=P(mem, head, None), check_vma=False
    )
```
